32 devices in a mesh: wide: 32 (over z, y, x, core), tensor: 1.
Axes of the slice: x: 2, y: 2, z: 4, core: 2. Of those that a mesh axis runs over, the one named last changes fastest.
Arguments:
- hidden: bfloat16 [49152, 3072], P('wide', 'tensor'), may hold values from -6 to 6
- modulation: float32 [2, 3072], P(None, 'tensor'), may hold values from -3 to 3
- final_weight: bfloat16 [3072, 64], P('tensor'), may hold values from -0.109375 to 0.109375
- noisy: float32 [49152, 64], P('wide'), may hold values from -6 to 6
- step_index: int32 [1], replicated, may hold values from 1 to 28
- slab_table: int32 [768], P('wide'), may hold values from 0 to 31, as said below
- conv_in_weight: bfloat16 [144, 512], P(None, 'tensor'), may hold values from -0.5 to 0.5
- conv_in_bias: float32 [512], P('tensor'), may hold values from -3 to 3
- conv1_weight: bfloat16 [9, 512, 512], replicated, may hold values from -0.09375 to 0.09375
- conv1_bias: float32 [512], replicated, may hold values from -3 to 3
Outputs:
- decoder_features: bfloat16 [1536, 512, 128], P('wide', 'tensor')
- residual_branch: bfloat16 [1536, 512, 128], P('wide', 'tensor')
The draws below stay inside these ranges and needn't reach their ends.
Inputs may be any that keep to these rules, and one draw needn't show every extreme that they name: There are 24 distinct offsets o_j, one per local row j, with slab_table[w * 24 + j] = (w - o_j) modulo the number of wide devices: each slab receives each local row index from exactly one wide device, and the rows of one device go to distinct slabs. One of the offsets is half the number of wide devices (rounded down).
All inputs are finite; a program needn't handle non-finite values.
Results may differ from the reference program's by a relative error of at most 0.012.
Values may be sent and summed in bfloat16 or wider, within the bound.
A program may use at most 192 MiB of HBM per device.

```python
import jax
import jax.numpy as jnp
from jax import lax

D = 3072
LC = 16
COUT = 512
GRID = 64
STEPS = 28
ROWS_DEV = 24
P_SIZE = 64
WPIX = 128
TOKEN_ROWS = 768
TOKENS = 49152
PIXROWS = 1536
IMAGES = 12


def draw_slab_table(key, part):
    slabs = TOKEN_ROWS // ROWS_DEV
    half = slabs // 2
    steps_away = jax.random.permutation(jax.random.fold_in(key, 1), slabs - 1)[:ROWS_DEV - 1].astype(jnp.int32) + 1
    chosen = jnp.concatenate([jnp.zeros((1,), jnp.int32), steps_away])
    offsets = (half + chosen) % slabs
    order = jax.random.permutation(jax.random.fold_in(key, 2), ROWS_DEV).astype(jnp.int32)
    offsets = offsets[order].astype(jnp.int32)
    owners = jnp.arange(slabs, dtype=jnp.int32)[:, None]
    return ((owners - offsets[None, :]) % slabs).reshape(-1).astype(jnp.int32)


def block_levels(rng, extent, shards, least, top_value):
    factor_of = 1.0
    for axis_at, parts in shards:
        steps = jax.random.uniform(jax.random.fold_in(jax.random.fold_in(rng, 6), axis_at), (parts,), jnp.float32, least / len(shards), top_value / len(shards))
        factor_of = factor_of * jnp.repeat(jnp.exp(steps), extent[axis_at] // parts).reshape((-1,) + (1,) * (len(extent) - 1 - axis_at))
    return factor_of


def bell_draw(key, shape, scale, most, pieces=(), kind=jnp.bfloat16):
    loudness = block_levels(key, shape, pieces, -0.22, 0.18) if pieces else 1.0
    drawn = jax.random.normal(key, shape, jnp.float32) * scale * loudness
    return jnp.minimum(jnp.maximum(drawn, -most), most).astype(kind)


def setup_inputs(seed: int = 0) -> dict:
    seeds = jax.random.split(jax.random.key(seed), 11)
    hidden = bell_draw(seeds[0], (TOKENS, D), 1.0, 6.0, ((0, 32),))
    modulation = bell_draw(seeds[1], (2, D), 0.5, 3.0, (), jnp.float32)
    final_weight = bell_draw(seeds[2], (D, P_SIZE), D ** -0.5, 0.109375)
    noisy = bell_draw(seeds[3], (TOKENS, P_SIZE), 1.0, 6.0, ((0, 32),), jnp.float32)
    step_index = jax.random.randint(seeds[4], (1,), 1, STEPS + 1).astype(jnp.int32)
    slab_table = draw_slab_table(jax.random.fold_in(seeds[10], 71), 0)
    conv_in_weight = bell_draw(seeds[6], (9 * LC, COUT), (9 * LC) ** -0.5, 0.5)
    conv_in_bias = bell_draw(seeds[7], (COUT,), 0.5, 3.0, (), jnp.float32)
    conv1_weight = bell_draw(seeds[8], (9, COUT, COUT), (9 * COUT) ** -0.5, 0.09375)
    conv1_bias = bell_draw(seeds[9], (COUT,), 0.5, 3.0, (), jnp.float32)
    return {"hidden": hidden, "modulation": modulation, "final_weight": final_weight, "noisy": noisy, "step_index": step_index, "slab_table": slab_table, "conv_in_weight": conv_in_weight, "conv_in_bias": conv_in_bias, "conv1_weight": conv1_weight, "conv1_bias": conv1_bias}


shift_value = 3.0
norm_eps = 1e-06

def image_conv(images, kernel):
    return lax.conv_general_dilated(images, kernel, (1, 1), 'SAME', dimension_numbers=('NHWC', 'HWIO', 'NHWC'), precision=lax.Precision.HIGHEST)

def reference(hidden, modulation, final_weight, noisy, step_index, slab_table, conv_in_weight, conv_in_bias, conv1_weight, conv1_bias):
    feats = hidden.astype(jnp.float32)
    mean = lax.optimization_barrier(jnp.mean(feats, axis=-1, keepdims=True))
    var = lax.optimization_barrier(jnp.mean(feats * feats, axis=-1, keepdims=True)) - mean * mean
    rstd = 1.0 / jnp.sqrt(var + norm_eps)
    normed = (feats - mean) * rstd * (1.0 + modulation[1]) + modulation[0]
    velocity = jnp.dot(normed, final_weight.astype(jnp.float32), precision=lax.Precision.HIGHEST)
    frac = step_index[0].astype(jnp.float32) / STEPS
    sigma = shift_value * frac / (1.0 + (shift_value - 1.0) * frac)
    clean = (noisy - sigma * velocity).astype(jnp.bfloat16)
    rows = clean.reshape(TOKEN_ROWS, GRID * P_SIZE)
    local_row = (jnp.arange(TOKEN_ROWS) % ROWS_DEV).astype(jnp.int32)
    target = slab_table.astype(jnp.int32) * ROWS_DEV + local_row
    ordered = jnp.zeros_like(rows).at[target].set(rows)
    latent_image = ordered.reshape(TOKEN_ROWS, GRID, 2, 2, LC).transpose(0, 2, 1, 3, 4).reshape(IMAGES, WPIX, WPIX, LC)
    kernel_in = conv_in_weight.astype(jnp.float32).reshape(3, 3, LC, COUT)
    first = image_conv(latent_image.astype(jnp.float32), kernel_in) + conv_in_bias
    features = first.astype(jnp.bfloat16)
    activated = jax.nn.silu(features.astype(jnp.float32)).astype(jnp.bfloat16)
    kernel_one = conv1_weight.astype(jnp.float32).reshape(3, 3, COUT, COUT)

    def one_image(image):
        return (image_conv(image[None].astype(jnp.float32), kernel_one)[0] + conv1_bias).astype(jnp.bfloat16)
    second = lax.map(one_image, activated)
    decoder_features = features.transpose(0, 1, 3, 2).reshape(PIXROWS, COUT, WPIX)
    residual_branch = second.transpose(0, 1, 3, 2).reshape(PIXROWS, COUT, WPIX)
    return (decoder_features, residual_branch)
```

```python
import functools

import jax
import jax.numpy as jnp
from jax import lax
from jax.experimental import pallas as pl
from jax.experimental.pallas import tpu as pltpu
from jax.sharding import PartitionSpec as P

D = 3072
LC = 16
GRID = 64
STEPS = 28
WPIX = 2 * GRID
PAIRS = 8

shift_value = 3.0
norm_eps = 1e-06
f32 = jnp.float32
bf16 = jnp.bfloat16
TRANS_B = (((1,), (1,)), ((), ()))


def split3(x):
    hi = x.astype(bf16)
    rest = x - hi.astype(f32)
    mid = rest.astype(bf16)
    return hi, mid, (rest - mid.astype(f32)).astype(bf16)


def project_kernel(features, sigma_ref, mod_ref, wt_ref, hidden_ref, noisy_ref, out_ref, wcat, consts):
    values = wt_ref.shape[0]

    @pl.when(pl.program_id(0) == 0)
    def _():
        wt = wt_ref[...]
        parts = split3(wt.astype(f32) * (1.0 + mod_ref[1:2, :]))
        for i, part in enumerate(parts):
            wcat[i * values : (i + 1) * values, :] = part
        wcat[3 * values :, :] = jnp.ones((values, wt.shape[1]), bf16)
        ones = jnp.ones((16, wt.shape[1]), bf16)
        sums = lax.dot_general(ones, wcat[...], TRANS_B, preferred_element_type=f32)
        total = sums[:, :values] + sums[:, values : 2 * values] + sums[:, 2 * values : 3 * values]
        shift = jnp.zeros((16, values), f32)
        for part in split3(jnp.broadcast_to(mod_ref[0:1, :], (16, wt.shape[1]))):
            shift = shift + lax.dot_general(part, wt, TRANS_B, preferred_element_type=f32)
        consts[0:1, :] = total[0:1, :]
        consts[1:2, :] = shift[0:1, :]

    h = hidden_ref[...]
    acc = lax.dot_general(h, wcat[...], TRANS_B, preferred_element_type=f32)
    hf = h.astype(f32)
    square = jnp.sum(hf * hf, axis=-1, keepdims=True)
    hw = acc[:, :values] + acc[:, values : 2 * values] + acc[:, 2 * values : 3 * values]
    mean = acc[:, 3 * values : 3 * values + 1] / features
    rstd = 1.0 / jnp.sqrt(square / features - mean * mean + norm_eps)
    velocity = rstd * (hw - mean * consts[0:1, :]) + consts[1:2, :]
    out_ref[...] = (noisy_ref[...] - sigma_ref[0:1, :] * velocity).astype(bf16)


def project(hidden, modulation, final_weight, noisy, sigma):
    tokens, features = hidden.shape
    values = final_weight.shape[1]
    block = 256
    return pl.pallas_call(
        functools.partial(project_kernel, features),
        grid=(tokens // block,),
        in_specs=[
            pl.BlockSpec((1, values), lambda i: (0, 0)),
            pl.BlockSpec((2, features), lambda i: (0, 0)),
            pl.BlockSpec((values, features), lambda i: (0, 0)),
            pl.BlockSpec((block, features), lambda i: (i, 0)),
            pl.BlockSpec((block, values), lambda i: (i, 0)),
        ],
        out_specs=pl.BlockSpec((block, values), lambda i: (i, 0)),
        out_shape=jax.ShapeDtypeStruct((tokens, values), bf16),
        scratch_shapes=[pltpu.VMEM((4 * values, features), bf16), pltpu.VMEM((8, values), f32)],
        compiler_params=pltpu.CompilerParams(vmem_limit_bytes=40 << 20),
        cost_estimate=pl.CostEstimate(flops=2 * tokens * features * 256, bytes_accessed=2 * tokens * features, transcendentals=0),
        name="project",
    )(jnp.broadcast_to(sigma, (1, values)), modulation, final_weight.T, hidden, noisy)


def decode_kernel(pairs, mask_ref, patch_ref, win_ref, bin_ref, u_ref, b1_ref, feat_ref, res_ref, act, pad, tr):
    step = pl.program_id(0)
    width = WPIX
    chans = win_ref.shape[1]
    rows = 2 * pairs
    chunk = 6

    @pl.when(step == 0)
    def _():
        pad[:, 0:8, :] = jnp.zeros((chunk, 8, chans), f32)
        pad[:, 8 + width :, :] = jnp.zeros((chunk, 8, chans), f32)

    def first(c, carry):
        base = pl.multiple_of((step * rows + c * chunk) * width, width)
        x = patch_ref[pl.ds(base, chunk * width), :]
        f = jnp.dot(x, win_ref[...], preferred_element_type=f32) + bin_ref[...]
        for q in range(chunk):
            fb = f[q * width : (q + 1) * width, :].astype(bf16)
            row = c * chunk + q
            fr = fb.astype(f32)

            @pl.when((row >= 1) & (row <= rows))
            def _():
                feat_ref[row - 1] = fr.T.astype(bf16)

            half = 0.5 * fr
            a = half + half * jnp.tanh(half)
            pad[q, 8 : 8 + width, :] = a
            act[row, :, chans : 2 * chans] = a.astype(bf16)
            act[row, :, 0:chans] = pad[q, 7 : 7 + width, :].astype(bf16)
            act[row, :, 2 * chans :] = pad[q, 9 : 9 + width, :].astype(bf16)
        return carry

    lax.fori_loop(0, (rows + 2) // chunk, first, 0)

    def transform(p, carry):
        at = pl.ds(pl.multiple_of(p * width, width), width)
        upper = mask_ref[0, step * pairs + p]
        lower = mask_ref[1, step * pairs + p]
        d1 = act[2 * p + 1]
        d2 = act[2 * p + 2]
        tr[1, at, :] = d1 + d2
        tr[2, at, :] = d2 - d1
        tr[0, at, :] = (act[2 * p].astype(f32) * upper - d2.astype(f32)).astype(bf16)
        tr[3, at, :] = (d1.astype(f32) - act[2 * p + 3].astype(f32) * lower).astype(bf16)
        return carry

    lax.fori_loop(0, pairs, transform, 0)

    tile = 256
    for n in range(chans // tile):
        cols = slice(n * tile, (n + 1) * tile)
        bias = b1_ref[:, cols]
        m = [jnp.dot(tr[k], u_ref[k, :, cols], preferred_element_type=f32) for k in range(4)]
        y0 = m[0] + (m[1] + m[2]) + bias
        y1 = (m[1] - m[2]) - m[3] + bias
        for p in range(pairs):
            at = slice(p * width, (p + 1) * width)
            res_ref[2 * p, cols, :] = y0[at].T.astype(bf16)
            res_ref[2 * p + 1, cols, :] = y1[at].T.astype(bf16)


def decode(masks, patches, win, b_in, u, b1, height):
    chans = win.shape[1]
    rows = 2 * PAIRS
    whole = lambda *shape: pl.BlockSpec(shape, lambda i: (0,) * len(shape), pipeline_mode=pl.Buffered(1))
    shape = jax.ShapeDtypeStruct((height, chans, WPIX), bf16)
    out = pl.BlockSpec((rows, chans, WPIX), lambda i: (i, 0, 0))
    return pl.pallas_call(
        functools.partial(decode_kernel, PAIRS),
        grid=(height // rows,),
        in_specs=[
            pl.BlockSpec(memory_space=pltpu.SMEM),
            whole(*patches.shape),
            whole(*win.shape),
            whole(1, chans),
            whole(*u.shape),
            whole(1, chans),
        ],
        out_specs=[out, out],
        out_shape=[shape, shape],
        scratch_shapes=[
            pltpu.VMEM((rows + 2, WPIX, 3 * chans), bf16),
            pltpu.VMEM((6, WPIX + 16, chans), f32),
            pltpu.VMEM((4, PAIRS * WPIX, 3 * chans), bf16),
        ],
        compiler_params=pltpu.CompilerParams(vmem_limit_bytes=60 << 20),
        cost_estimate=pl.CostEstimate(flops=height * WPIX * 12 * 512 * 512, bytes_accessed=30 << 20, transcendentals=0),
        name="decode",
    )(masks, patches, win, b_in[None], u, b1[None])


def edge_masks(first_row, count, height):
    global_rows = first_row + jnp.arange(count, dtype=jnp.int32)
    upper = (global_rows % height != 0).astype(f32)
    lower = (global_rows % height != height - 1).astype(f32)
    return (upper, jnp.ones_like(upper), lower)


def padded_2(value, axis, width):
    count, length = (lax.axis_size(axis), value.shape[0])
    up = [(i, (i + 1) % count) for i in range(count - 1)]
    down = [(j, i) for i, j in up]
    before = lax.ppermute(value[length - width :], axis, up)
    after = lax.ppermute(value[:width], axis, down)
    return jnp.concatenate([before, value, after], axis=0)


def patches_of(latent, first_row, count):
    planes = latent.reshape(latent.shape[0], WPIX, LC)
    padded = jnp.pad(planes, ((0, 0), (1, 1), (0, 0)))
    masks = edge_masks(first_row, count, WPIX)
    pieces = []
    for row_off in range(3):
        keep = masks[row_off].astype(bf16)[:, None, None]
        for col_off in range(3):
            pieces.append(padded[row_off : row_off + count, col_off : col_off + WPIX, :] * keep)
    return jnp.concatenate(pieces, axis=-1).reshape(count * WPIX, 9 * LC)


def shards(hidden, modulation, final_weight, noisy, step_index, slab_table, conv_in_weight, conv_in_bias, conv1_weight, conv1_bias):
    frac = step_index[0].astype(f32) / STEPS
    sigma = shift_value * frac / (1.0 + (shift_value - 1.0) * frac)
    clean = project(hidden, modulation, final_weight, noisy, sigma)
    rows_here = slab_table.shape[0]
    token_rows = clean.reshape(rows_here, -1)
    slabs = lax.axis_size("wide")
    slab_here = lax.axis_index("wide")
    slab_ids = jnp.arange(slabs, dtype=jnp.int32)
    outgoing = (slab_ids[:, None] == slab_table[None, :]).astype(bf16)
    sendbuf = jnp.dot(outgoing, token_rows, preferred_element_type=f32).astype(bf16)
    received = lax.all_to_all(sendbuf, "wide", split_axis=0, concat_axis=0, tiled=True)
    g = conv1_weight.reshape(3, 3 * conv1_weight.shape[1], conv1_weight.shape[2])
    gf = g.astype(f32)
    u = jnp.stack([g[0], (0.5 * (gf[0] + gf[1] + gf[2])).astype(bf16), (0.5 * (gf[0] - gf[1] + gf[2])).astype(bf16), g[2]])
    source = (2 * slab_here - slab_table) % slabs
    incoming = (source[:, None] == slab_ids[None, :]).astype(bf16)
    slab_rows = jnp.dot(incoming, received, preferred_element_type=f32).astype(bf16)
    pixel_rows = slab_rows.reshape(rows_here, GRID, 2, 2, LC).transpose(0, 2, 1, 3, 4).reshape(2 * rows_here, WPIX * LC)
    latent = padded_2(pixel_rows, "wide", 2)
    height = 2 * rows_here
    patches = patches_of(latent, slab_here * height - 1, height + 2)
    tops = slab_here * height + 2 * jnp.arange(rows_here, dtype=jnp.int32)
    masks = jnp.stack([tops % WPIX != 0, (tops + 2) % WPIX != 0]).astype(f32)
    return tuple(decode(masks, patches, conv_in_weight, conv_in_bias, u, conv1_bias, height))


def split_padded(value, sides, width):
    for axis, dim in sides:
        count, length = (lax.axis_size(axis), value.shape[dim])
        up = [(i, (i + 1) % count) for i in range(count - 1)]
        down = [(j, i) for i, j in up]
        last = lax.slice_in_dim(value, length - width, length, axis=dim)
        first = lax.slice_in_dim(value, 0, width, axis=dim)
        before = lax.ppermute(last, axis, up)
        after = lax.ppermute(first, axis, down)
        value = jnp.concatenate([before, value, after], axis=dim)
    return value


def conv_input_rows(latent, weight, bias, first_row, count, channels):
    width = latent.shape[1] // channels
    planes = latent.reshape(latent.shape[0], width, channels)
    padded = jnp.pad(planes, ((0, 0), (1, 1), (0, 0)))
    masks = edge_masks(first_row, count, width)
    pieces = []
    for row_off in range(3):
        keep = masks[row_off].astype(jnp.bfloat16)[:, None, None]
        for col_off in range(3):
            pieces.append(padded[row_off : row_off + count, col_off : col_off + width, :] * keep)
    patches = jnp.concatenate(pieces, axis=-1)
    return jnp.einsum("rwk,ko->rwo", patches, weight, preferred_element_type=jnp.float32) + bias


def conv_three(total, inputs, weights, first_row, count):
    width = inputs.shape[2]
    padded = jnp.pad(inputs, ((0, 0), (0, 0), (1, 1)))
    masks = edge_masks(first_row, count, width)
    for row_off in range(3):
        keep = masks[row_off][:, None, None]
        for col_off in range(3):
            window = padded[row_off : row_off + count, :, col_off : col_off + width]
            term = jnp.einsum(
                "rkw,ko->row",
                window,
                weights[3 * row_off + col_off],
                preferred_element_type=jnp.float32,
            )
            total = total + keep * term
    return total


def split_shards(
    hidden,
    modulation,
    final_weight,
    noisy,
    step_index,
    slab_table,
    conv_in_weight,
    conv_in_bias,
    conv1_weight,
    conv1_bias,
):
    feats = hidden.astype(jnp.float32)
    weight_f = final_weight.astype(jnp.float32)
    width_all = D
    first_sum, square_sum = lax.psum(
        (jnp.sum(feats, axis=-1), jnp.sum(feats * feats, axis=-1)), "tensor"
    )
    mean = first_sum / width_all
    rstd = 1.0 / jnp.sqrt(square_sum / width_all - mean * mean + norm_eps)
    normed = (feats - mean[:, None]) * rstd[:, None] * (1.0 + modulation[1]) + modulation[0]
    partial_proj = jnp.dot(normed, weight_f, precision=lax.Precision.HIGHEST)
    velocity = lax.psum(partial_proj, "tensor")
    frac = step_index[0].astype(jnp.float32) / STEPS
    sigma = shift_value * frac / (1.0 + (shift_value - 1.0) * frac)
    clean = (noisy - sigma * velocity).astype(jnp.bfloat16)
    rows_here = slab_table.shape[0]
    token_rows = clean.reshape(rows_here, -1)
    slabs = lax.axis_size("wide")
    slab_here = lax.axis_index("wide")
    slab_ids = jnp.arange(slabs, dtype=jnp.int32)
    outgoing = (slab_ids[:, None] == slab_table[None, :]).astype(jnp.bfloat16)
    sendbuf = jnp.dot(outgoing, token_rows, preferred_element_type=jnp.float32).astype(jnp.bfloat16)
    received = lax.all_to_all(sendbuf, "wide", split_axis=0, concat_axis=0, tiled=True)
    source = (2 * slab_here - slab_table) % slabs
    incoming = (source[:, None] == slab_ids[None, :]).astype(jnp.bfloat16)
    slab_rows = jnp.dot(incoming, received, preferred_element_type=jnp.float32).astype(jnp.bfloat16)
    grid_side = GRID
    channels = LC
    pixel_rows = (
        slab_rows.reshape(rows_here, grid_side, 2, 2, channels)
        .transpose(0, 2, 1, 3, 4)
        .reshape(2 * rows_here, 4 * grid_side * channels // 2)
    )
    depth = 2
    latent = split_padded(pixel_rows, (("wide", 0),), depth)
    slab_height = 2 * rows_here
    conv_rows = slab_height + 2 * (depth - 1)
    first_conv = slab_here * slab_height - (depth - 1)
    first = conv_input_rows(latent, conv_in_weight, conv_in_bias, first_conv, conv_rows, channels)
    features = first.astype(jnp.bfloat16).transpose(0, 2, 1)
    activated = jax.nn.silu(features.astype(jnp.float32)).astype(jnp.bfloat16)
    decoder_features = features[depth - 1 : depth - 1 + slab_height]
    local_out = conv_in_weight.shape[1]
    tensor_here = lax.axis_index("tensor")
    pixel_width = activated.shape[2]
    columns = lax.dynamic_slice_in_dim(conv1_weight, tensor_here * local_out, local_out, 2)
    bias_part = lax.dynamic_slice_in_dim(conv1_bias, tensor_here * local_out, local_out, 0)
    first_out = slab_here * slab_height
    gathered = lax.all_gather(activated, "tensor", axis=1, tiled=True)
    start_total = jnp.zeros((slab_height, local_out, pixel_width), jnp.float32)
    summed = conv_three(start_total, gathered, columns, first_out, slab_height)
    residual_branch = (summed + bias_part[None, :, None]).astype(jnp.bfloat16)
    return (decoder_features, residual_branch)


def solution(mesh):
    whole_channels = mesh.shape["tensor"] == 1
    return jax.shard_map(
        shards if whole_channels else split_shards,
        mesh=mesh,
        in_specs=(
            P("wide", "tensor"),
            P(None, "tensor"),
            P("tensor", None),
            P("wide", None),
            P(),
            P("wide"),
            P(None, "tensor"),
            P("tensor"),
            P(),
            P(),
        ),
        out_specs=(P("wide", "tensor", None), P("wide", "tensor", None)),
        check_vma=False,
    )
```

```python
import functools

import jax
import jax.numpy as jnp
import numpy as np
from jax import lax
from jax.experimental import pallas as pl
from jax.experimental.pallas import tpu as pltpu
from jax.sharding import PartitionSpec as P

D = 3072
LC = 16
GRID = 64
STEPS = 28
WPIX = 2 * GRID
HALF = GRID // 2
CHUNK = 4
MESH = pl.DeviceIdType.MESH

shift_value = 3.0
norm_eps = 1e-06
f32 = jnp.float32
bf16 = jnp.bfloat16
TRANS_B = (((1,), (1,)), ((), ()))


def split3(x):
    hi = x.astype(bf16)
    rest = x - hi.astype(f32)
    mid = rest.astype(bf16)
    return hi, mid, (rest - mid.astype(f32)).astype(bf16)


def relay_kernel(slabs, features, inv_ref, src_ref, sigma_ref, mod_ref, wt_ref, hidden_ref, noisy_ref, x_ref, wcat, consts, rows, sendbuf, recv, ordered, halo, shifted, wide, send_sem, recv_sem, edge_send, edge_recv):
    step = pl.program_id(0)
    me = lax.axis_index("wide")
    values = wt_ref.shape[0]
    count = rows.shape[0]
    barrier = pltpu.get_barrier_semaphore()

    @pl.when(step == 0)
    def _():
        for k in range(1, slabs):
            pl.semaphore_signal(barrier, inc=1, device_id={"wide": lax.rem(me + k, slabs)}, device_id_type=MESH)
        wt = wt_ref[...]
        parts = split3(wt.astype(f32) * (1.0 + mod_ref[1:2, :]))
        for i, part in enumerate(parts):
            wcat[i * values : (i + 1) * values, :] = part
        wcat[3 * values :, :] = jnp.ones((values, wt.shape[1]), bf16)
        ones = jnp.ones((16, wt.shape[1]), bf16)
        sums = lax.dot_general(ones, wcat[...], TRANS_B, preferred_element_type=f32)
        total = sums[:, :values] + sums[:, values : 2 * values] + sums[:, 2 * values : 3 * values]
        shift = jnp.zeros((16, values), f32)
        for part in split3(jnp.broadcast_to(mod_ref[0:1, :], (16, wt.shape[1]))):
            shift = shift + lax.dot_general(part, wt, TRANS_B, preferred_element_type=f32)
        consts[0:1, :] = total[0:1, :]
        consts[1:2, :] = shift[0:1, :]

    h = hidden_ref[...]
    acc = lax.dot_general(h, wcat[...], TRANS_B, preferred_element_type=f32)
    hf = h.astype(f32)
    square = jnp.sum(hf * hf, axis=-1, keepdims=True)
    hw = acc[:, :values] + acc[:, values : 2 * values] + acc[:, 2 * values : 3 * values]
    mean = acc[:, 3 * values : 3 * values + 1] / features
    rstd = 1.0 / jnp.sqrt(square / features - mean * mean + norm_eps)
    velocity = rstd * (hw - mean * consts[0:1, :]) + consts[1:2, :]
    clean = noisy_ref[...] - sigma_ref[0:1, :] * velocity
    here = h.shape[0] // GRID
    for t in range(here):
        pair = [clean[t * GRID : t * GRID + HALF], clean[t * GRID + HALF : (t + 1) * GRID]]
        rows[step * here + t] = jnp.concatenate(pair, axis=1).astype(bf16)

    @pl.when(step == pl.num_programs(0) - 1)
    def _():
        pl.semaphore_wait(barrier, slabs - 1)
        for d in range(slabs):
            sendbuf[d] = rows[inv_ref[d]]
        copies = []
        for k in range(1, slabs):
            peer = lax.rem(me + k, slabs)
            copy = pltpu.make_async_remote_copy(
                src_ref=sendbuf.at[peer],
                dst_ref=recv.at[me],
                send_sem=send_sem.at[k],
                recv_sem=recv_sem.at[k],
                device_id={"wide": peer},
                device_id_type=MESH,
            )
            copy.start()
            copies.append(copy)
        recv[me] = sendbuf[me]
        for copy in copies:
            copy.wait_recv()
        for j in range(count):
            ordered[j] = recv[src_ref[j]]
        edges = []
        for e, (row, peer) in enumerate(((count - 1, lax.rem(me + 1, slabs)), (0, lax.rem(me + slabs - 1, slabs)))):
            copy = pltpu.make_async_remote_copy(
                src_ref=ordered.at[row],
                dst_ref=halo.at[e],
                send_sem=edge_send.at[e],
                recv_sem=edge_recv.at[e],
                device_id={"wide": peer},
                device_id_type=MESH,
            )
            copy.start()
            edges.append(copy)

        lane = lax.broadcasted_iota(jnp.int32, (GRID, 2 * GRID), 1)
        own = lane < GRID
        from_left = (lane // LC) % 2 == 1
        from_upper = (lane // (2 * LC)) % 2 == 1
        zeros = jnp.zeros((8, 2 * GRID), f32)

        def widen(packed, at):
            p = packed.astype(f32)
            swapped = jnp.concatenate([p[:, GRID:], p[:, :GRID]], axis=1)
            twice = jnp.concatenate([jnp.where(own[:HALF], p, swapped), jnp.where(own[:HALF], swapped, p)], axis=0)
            shifted[at, 0:8, :] = zeros
            shifted[at, 8 : 8 + GRID, :] = twice
            shifted[at, 8 + GRID :, :] = zeros
            beside = jnp.where(from_left, shifted[at, 7 : 7 + GRID, :], shifted[at, 9 : 9 + GRID, :])
            wide[at] = jnp.where(own, twice, beside)

        for j in range(count):
            widen(ordered[j], j + 1)
        for copy in edges:
            copy.wait_recv()
        widen(halo[0], 0)
        widen(halo[1], count + 1)
        for i in range(count + 2):
            first = me * count + i - 1 + GRID
            upper = jnp.where(lax.rem(first, GRID) != 0, 1.0, 0.0).astype(f32)
            lower = jnp.where(lax.rem(first + 1, GRID) != 0, 1.0, 0.0).astype(f32)
            above = wide[max(i - 1, 0)] * upper
            below = wide[min(i + 1, count + 1)] * lower
            x_ref[i * GRID : (i + 1) * GRID, 0 : 2 * GRID] = wide[i].astype(bf16)
            x_ref[i * GRID : (i + 1) * GRID, 2 * GRID :] = jnp.where(from_upper, above, below).astype(bf16)
        for copy in copies + edges:
            copy.wait_send()


def relay(hidden, modulation, final_weight, noisy, sigma, inverse, source, slabs):
    tokens, features = hidden.shape
    values = final_weight.shape[1]
    count = source.shape[0]
    block = 256
    smem = pl.BlockSpec(memory_space=pltpu.SMEM)
    row = (HALF, 2 * values)
    return pl.pallas_call(
        functools.partial(relay_kernel, slabs, features),
        grid=(tokens // block,),
        in_specs=[
            smem,
            smem,
            pl.BlockSpec((1, values), lambda i: (0, 0)),
            pl.BlockSpec((2, features), lambda i: (0, 0)),
            pl.BlockSpec((values, features), lambda i: (0, 0)),
            pl.BlockSpec((block, features), lambda i: (i, 0)),
            pl.BlockSpec((block, values), lambda i: (i, 0)),
        ],
        out_specs=pl.BlockSpec(((count + 2) * GRID, 4 * values), lambda i: (0, 0)),
        out_shape=jax.ShapeDtypeStruct(((count + 2) * GRID, 4 * values), bf16),
        scratch_shapes=[
            pltpu.VMEM((4 * values, features), bf16),
            pltpu.VMEM((8, values), f32),
            pltpu.VMEM((count,) + row, bf16),
            pltpu.VMEM((slabs,) + row, bf16),
            pltpu.VMEM((slabs,) + row, bf16),
            pltpu.VMEM((count,) + row, bf16),
            pltpu.VMEM((2,) + row, bf16),
            pltpu.VMEM((count + 2, GRID + 16, 2 * values), f32),
            pltpu.VMEM((count + 2, GRID, 2 * values), f32),
            pltpu.SemaphoreType.DMA((slabs,)),
            pltpu.SemaphoreType.DMA((slabs,)),
            pltpu.SemaphoreType.DMA((2,)),
            pltpu.SemaphoreType.DMA((2,)),
        ],
        compiler_params=pltpu.CompilerParams(vmem_limit_bytes=40 << 20, collective_id=0, has_side_effects=True),
        cost_estimate=pl.CostEstimate(flops=2 * tokens * features * 256, bytes_accessed=2 * tokens * features, transcendentals=0),
        name="relay",
    )(inverse, source, jnp.broadcast_to(sigma, (1, values)), modulation, final_weight.T, hidden, noisy)


def spread_table():
    table = np.zeros((4, 4 * GRID, 9 * LC), np.float32)
    for at in range(4 * GRID):
        lane = at % (2 * GRID)
        a, b, c = (lane // (2 * LC)) % 2, (lane // LC) % 2, lane % LC
        row = a if at < 2 * GRID else (a - 2 if a == 1 else a + 2)
        col = b if lane < GRID else (b - 2 if b == 1 else b + 2)
        for pixel in range(4):
            dr, dc = row - pixel // 2 + 1, col - pixel % 2 + 1
            if 0 <= dr < 3 and 0 <= dc < 3:
                table[pixel, at, (3 * dr + dc) * LC + c] = 1.0
    return table.reshape(-1, 9 * LC)


def decode_kernel(mask_ref, x_ref, spread_ref, win_ref, bin_ref, g_ref, b1_ref, feat_ref, res_ref, wbig, mixed, nat, pad, act, tr_a, tr_b):
    step = pl.program_id(0)
    last = pl.num_programs(0) - 1
    chans = win_ref.shape[1]
    patch = x_ref.shape[1]
    pixel_rows = 2 * CHUNK
    tile = 256

    def setup():
        pad[:, 0:8, :] = jnp.zeros((pixel_rows + 2, 8, chans), f32)
        pad[:, 8 + WPIX :, :] = jnp.zeros((pixel_rows + 2, 8, chans), f32)
        for pixel in range(4):
            part = spread_ref[pixel * patch : (pixel + 1) * patch, :]
            wbig[pixel] = jnp.dot(part, win_ref[...], preferred_element_type=f32).astype(bf16)

        def mix(i, carry):
            at = pl.ds(pl.multiple_of(i * 64, 64), 64)
            outer = 0.5 * (g_ref[0, at, :].astype(f32) + g_ref[2, at, :].astype(f32))
            inner = 0.5 * g_ref[1, at, :].astype(f32)
            mixed[0, at, :] = (outer + inner).astype(bf16)
            mixed[1, at, :] = (outer - inner).astype(bf16)
            return carry

        lax.fori_loop(0, g_ref.shape[1] // 64, mix, 0)

    def prepare(tr):
        base = step * CHUNK * GRID

        def first(start, length, pixel):
            x = x_ref[pl.ds(pl.multiple_of(start, GRID), length), :]
            f = jnp.dot(x, wbig[pixel], preferred_element_type=f32) + bin_ref[...]
            return f.astype(bf16).astype(f32)

        def keep(f, row, b):
            for c in range(chans // 128):
                nat[row, c, pl.ds(b, GRID, stride=2), :] = f[:, c * 128 : (c + 1) * 128]

        for b in range(2):
            keep(first(base, GRID, 2 + b), 0, b)
            keep(first(base + (CHUNK + 1) * GRID, GRID, b), pixel_rows + 1, b)
        for pixel in range(4):
            f = first(base + GRID, CHUNK * GRID, pixel)
            for t in range(CHUNK):
                keep(f[t * GRID : (t + 1) * GRID], 1 + 2 * t + pixel // 2, pixel % 2)
        for r in range(pixel_rows + 2):
            f = jnp.concatenate([nat[r, c] for c in range(chans // 128)], axis=1)
            if 1 <= r <= pixel_rows:
                feat_ref[r - 1] = f.astype(bf16).T
            half = 0.5 * f
            a = half + half * jnp.tanh(half)
            if r == 0:
                a = a * mask_ref[0, step]
            if r == pixel_rows + 1:
                a = a * mask_ref[1, step]
            pad[r, 8 : 8 + WPIX, :] = a
            act[r, :, chans : 2 * chans] = a.astype(bf16)
            act[r, :, 0:chans] = pad[r, 7 : 7 + WPIX, :].astype(bf16)
            act[r, :, 2 * chans :] = pad[r, 9 : 9 + WPIX, :].astype(bf16)
        for p in range(CHUNK):
            at = slice(p * WPIX, (p + 1) * WPIX)
            d = [act[2 * p + i] for i in range(4)]
            tr[0, at, :] = d[0] - d[2]
            tr[1, at, :] = d[1] + d[2]
            tr[2, at, :] = d[2] - d[1]
            tr[3, at, :] = d[1] - d[3]

    def residual(tr):
        for n in range(chans // tile):
            cols = slice(n * tile, (n + 1) * tile)
            bias = b1_ref[:, cols]
            factors = (g_ref[0, :, cols], mixed[0, :, cols], mixed[1, :, cols], g_ref[2, :, cols])
            m = [jnp.dot(tr[k], factors[k], preferred_element_type=f32) for k in range(4)]
            y0 = m[0] + (m[1] + m[2]) + bias
            y1 = (m[1] - m[2]) - m[3] + bias
            for p in range(CHUNK):
                at = slice(p * WPIX, (p + 1) * WPIX)
                res_ref[2 * p, cols, :] = y0[at].astype(bf16).T
                res_ref[2 * p + 1, cols, :] = y1[at].astype(bf16).T

    @pl.when(step == 0)
    def _():
        setup()
        prepare(tr_a)

    @pl.when((step > 0) & (step < last) & (lax.rem(step, 2) == 1))
    def _():
        residual(tr_a)
        prepare(tr_b)

    @pl.when((step > 0) & (step < last) & (lax.rem(step, 2) == 0))
    def _():
        residual(tr_b)
        prepare(tr_a)

    @pl.when((step == last) & (lax.rem(step, 2) == 1))
    def _():
        residual(tr_a)

    @pl.when((step == last) & (lax.rem(step, 2) == 0))
    def _():
        residual(tr_b)


def decode(masks, x, win, b_in, g, b1, height):
    chans = win.shape[1]
    rows = 2 * CHUNK
    steps = height // rows
    whole = lambda *shape: pl.BlockSpec(shape, lambda i: (0,) * len(shape), pipeline_mode=pl.Buffered(1))
    shape = jax.ShapeDtypeStruct((height, chans, WPIX), bf16)
    spread = jnp.asarray(spread_table(), bf16)
    return pl.pallas_call(
        decode_kernel,
        grid=(steps + 1,),
        in_specs=[
            pl.BlockSpec(memory_space=pltpu.SMEM),
            whole(*x.shape),
            whole(*spread.shape),
            whole(*win.shape),
            whole(1, chans),
            whole(*g.shape),
            whole(1, chans),
        ],
        out_specs=[
            pl.BlockSpec((rows, chans, WPIX), lambda i: (jnp.minimum(i, steps - 1), 0, 0)),
            pl.BlockSpec((rows, chans, WPIX), lambda i: (jnp.maximum(i - 1, 0), 0, 0)),
        ],
        out_shape=[shape, shape],
        scratch_shapes=[
            pltpu.VMEM((4, x.shape[1], chans), bf16),
            pltpu.VMEM((2,) + g.shape[1:], bf16),
            pltpu.VMEM((rows + 2, chans // 128, WPIX, 128), f32),
            pltpu.VMEM((rows + 2, WPIX + 16, chans), f32),
            pltpu.VMEM((rows + 2, WPIX, 3 * chans), bf16),
            pltpu.VMEM((4, CHUNK * WPIX, 3 * chans), bf16),
            pltpu.VMEM((4, CHUNK * WPIX, 3 * chans), bf16),
        ],
        compiler_params=pltpu.CompilerParams(vmem_limit_bytes=60 << 20),
        cost_estimate=pl.CostEstimate(flops=height * WPIX * 12 * 512 * 512, bytes_accessed=30 << 20, transcendentals=0),
        name="decode",
    )(masks, x, spread, win, b_in[None], g, b1[None])


def shards(hidden, modulation, final_weight, noisy, step_index, slab_table, conv_in_weight, conv_in_bias, conv1_weight, conv1_bias):
    frac = step_index[0].astype(f32) / STEPS
    sigma = shift_value * frac / (1.0 + (shift_value - 1.0) * frac)
    rows_here = slab_table.shape[0]
    slabs = lax.axis_size("wide")
    slab_here = lax.axis_index("wide")
    slab_ids = jnp.arange(slabs, dtype=jnp.int32)
    local = jnp.arange(rows_here, dtype=jnp.int32)
    inverse = jnp.sum(jnp.where(slab_ids[:, None] == slab_table[None, :], local[None, :], 0), axis=1)
    source = (2 * slab_here - slab_table) % slabs
    x = relay(hidden, modulation, final_weight, noisy, sigma, inverse, source, slabs)
    height = 2 * rows_here
    g = conv1_weight.reshape(3, 3 * conv1_weight.shape[1], conv1_weight.shape[2])
    tops = slab_here * height + 2 * CHUNK * jnp.arange(rows_here // CHUNK + 1, dtype=jnp.int32)
    masks = jnp.stack([tops % WPIX != 0, (tops + 2 * CHUNK) % WPIX != 0]).astype(f32)
    return tuple(decode(masks, x, conv_in_weight, conv_in_bias, g, conv1_bias, height))


def edge_masks(first_row, count, height):
    global_rows = first_row + jnp.arange(count, dtype=jnp.int32)
    upper = (global_rows % height != 0).astype(f32)
    lower = (global_rows % height != height - 1).astype(f32)
    return (upper, jnp.ones_like(upper), lower)


def split_padded(value, sides, width):
    for axis, dim in sides:
        count, length = (lax.axis_size(axis), value.shape[dim])
        up = [(i, (i + 1) % count) for i in range(count - 1)]
        down = [(j, i) for i, j in up]
        last = lax.slice_in_dim(value, length - width, length, axis=dim)
        first = lax.slice_in_dim(value, 0, width, axis=dim)
        before = lax.ppermute(last, axis, up)
        after = lax.ppermute(first, axis, down)
        value = jnp.concatenate([before, value, after], axis=dim)
    return value


def conv_input_rows(latent, weight, bias, first_row, count, channels):
    width = latent.shape[1] // channels
    planes = latent.reshape(latent.shape[0], width, channels)
    padded = jnp.pad(planes, ((0, 0), (1, 1), (0, 0)))
    masks = edge_masks(first_row, count, width)
    pieces = []
    for row_off in range(3):
        keep = masks[row_off].astype(jnp.bfloat16)[:, None, None]
        for col_off in range(3):
            pieces.append(padded[row_off : row_off + count, col_off : col_off + width, :] * keep)
    patches = jnp.concatenate(pieces, axis=-1)
    return jnp.einsum("rwk,ko->rwo", patches, weight, preferred_element_type=jnp.float32) + bias


def conv_three(total, inputs, weights, first_row, count):
    width = inputs.shape[2]
    padded = jnp.pad(inputs, ((0, 0), (0, 0), (1, 1)))
    masks = edge_masks(first_row, count, width)
    for row_off in range(3):
        keep = masks[row_off][:, None, None]
        for col_off in range(3):
            window = padded[row_off : row_off + count, :, col_off : col_off + width]
            term = jnp.einsum(
                "rkw,ko->row",
                window,
                weights[3 * row_off + col_off],
                preferred_element_type=jnp.float32,
            )
            total = total + keep * term
    return total


def split_shards(
    hidden,
    modulation,
    final_weight,
    noisy,
    step_index,
    slab_table,
    conv_in_weight,
    conv_in_bias,
    conv1_weight,
    conv1_bias,
):
    feats = hidden.astype(jnp.float32)
    weight_f = final_weight.astype(jnp.float32)
    width_all = D
    first_sum, square_sum = lax.psum(
        (jnp.sum(feats, axis=-1), jnp.sum(feats * feats, axis=-1)), "tensor"
    )
    mean = first_sum / width_all
    rstd = 1.0 / jnp.sqrt(square_sum / width_all - mean * mean + norm_eps)
    normed = (feats - mean[:, None]) * rstd[:, None] * (1.0 + modulation[1]) + modulation[0]
    partial_proj = jnp.dot(normed, weight_f, precision=lax.Precision.HIGHEST)
    velocity = lax.psum(partial_proj, "tensor")
    frac = step_index[0].astype(jnp.float32) / STEPS
    sigma = shift_value * frac / (1.0 + (shift_value - 1.0) * frac)
    clean = (noisy - sigma * velocity).astype(jnp.bfloat16)
    rows_here = slab_table.shape[0]
    token_rows = clean.reshape(rows_here, -1)
    slabs = lax.axis_size("wide")
    slab_here = lax.axis_index("wide")
    slab_ids = jnp.arange(slabs, dtype=jnp.int32)
    outgoing = (slab_ids[:, None] == slab_table[None, :]).astype(jnp.bfloat16)
    sendbuf = jnp.dot(outgoing, token_rows, preferred_element_type=jnp.float32).astype(jnp.bfloat16)
    received = lax.all_to_all(sendbuf, "wide", split_axis=0, concat_axis=0, tiled=True)
    source = (2 * slab_here - slab_table) % slabs
    incoming = (source[:, None] == slab_ids[None, :]).astype(jnp.bfloat16)
    slab_rows = jnp.dot(incoming, received, preferred_element_type=jnp.float32).astype(jnp.bfloat16)
    grid_side = GRID
    channels = LC
    pixel_rows = (
        slab_rows.reshape(rows_here, grid_side, 2, 2, channels)
        .transpose(0, 2, 1, 3, 4)
        .reshape(2 * rows_here, 4 * grid_side * channels // 2)
    )
    depth = 2
    latent = split_padded(pixel_rows, (("wide", 0),), depth)
    slab_height = 2 * rows_here
    conv_rows = slab_height + 2 * (depth - 1)
    first_conv = slab_here * slab_height - (depth - 1)
    first = conv_input_rows(latent, conv_in_weight, conv_in_bias, first_conv, conv_rows, channels)
    features = first.astype(jnp.bfloat16).transpose(0, 2, 1)
    activated = jax.nn.silu(features.astype(jnp.float32)).astype(jnp.bfloat16)
    decoder_features = features[depth - 1 : depth - 1 + slab_height]
    local_out = conv_in_weight.shape[1]
    tensor_here = lax.axis_index("tensor")
    pixel_width = activated.shape[2]
    columns = lax.dynamic_slice_in_dim(conv1_weight, tensor_here * local_out, local_out, 2)
    bias_part = lax.dynamic_slice_in_dim(conv1_bias, tensor_here * local_out, local_out, 0)
    first_out = slab_here * slab_height
    gathered = lax.all_gather(activated, "tensor", axis=1, tiled=True)
    start_total = jnp.zeros((slab_height, local_out, pixel_width), jnp.float32)
    summed = conv_three(start_total, gathered, columns, first_out, slab_height)
    residual_branch = (summed + bias_part[None, :, None]).astype(jnp.bfloat16)
    return (decoder_features, residual_branch)


def solution(mesh):
    whole_channels = mesh.shape["tensor"] == 1
    return jax.shard_map(
        shards if whole_channels else split_shards,
        mesh=mesh,
        in_specs=(
            P("wide", "tensor"),
            P(None, "tensor"),
            P("tensor", None),
            P("wide", None),
            P(),
            P("wide"),
            P(None, "tensor"),
            P("tensor"),
            P(),
            P(),
        ),
        out_specs=(P("wide", "tensor", None), P("wide", "tensor", None)),
        check_vma=False,
    )
```

```python
import functools

import jax
import jax.numpy as jnp
import numpy as np
from jax import lax
from jax.experimental import pallas as pl
from jax.experimental.pallas import tpu as pltpu
from jax.sharding import PartitionSpec as P

D = 3072
LC = 16
GRID = 64
STEPS = 28
WPIX = 2 * GRID
HALF = GRID // 2
CHUNK = 4
MESH = pl.DeviceIdType.MESH

shift_value = 3.0
norm_eps = 1e-06
f32 = jnp.float32
bf16 = jnp.bfloat16
TRANS_B = (((1,), (1,)), ((), ()))


def split3(x):
    hi = x.astype(bf16)
    rest = x - hi.astype(f32)
    mid = rest.astype(bf16)
    return hi, mid, (rest - mid.astype(f32)).astype(bf16)


def relay_kernel(slabs, features, inv_ref, table_ref, sigma_ref, mod_ref, wt_ref, hidden_ref, noisy_ref, g_ref, x_ref, mixed_ref, wcat, consts, rows, sendbuf, recv, ordered, halo, shifted, wide, send_sem, recv_sem, edge_send, edge_recv):
    step = pl.program_id(0)
    me = lax.axis_index("wide")
    values = wt_ref.shape[0]
    count = rows.shape[0]
    barrier = pltpu.get_barrier_semaphore()

    @pl.when(step == 0)
    def _():
        for k in range(1, slabs):
            pl.semaphore_signal(barrier, inc=1, device_id={"wide": lax.rem(me + k, slabs)}, device_id_type=MESH)
        wt = wt_ref[...]
        parts = split3(wt.astype(f32) * (1.0 + mod_ref[1:2, :]))
        for i, part in enumerate(parts):
            wcat[i * values : (i + 1) * values, :] = part
        wcat[3 * values :, :] = jnp.ones((values, wt.shape[1]), bf16)
        ones = jnp.ones((16, wt.shape[1]), bf16)
        sums = lax.dot_general(ones, wcat[...], TRANS_B, preferred_element_type=f32)
        total = sums[:, :values] + sums[:, values : 2 * values] + sums[:, 2 * values : 3 * values]
        shift = jnp.zeros((16, values), f32)
        for part in split3(jnp.broadcast_to(mod_ref[0:1, :], (16, wt.shape[1]))):
            shift = shift + lax.dot_general(part, wt, TRANS_B, preferred_element_type=f32)
        consts[0:1, :] = total[0:1, :]
        consts[1:2, :] = shift[0:1, :]

    h = hidden_ref[...]
    acc = lax.dot_general(h, wcat[...], TRANS_B, preferred_element_type=f32)
    hf = h.astype(f32)
    square = jnp.sum(hf * hf, axis=-1, keepdims=True)
    hw = acc[:, :values] + acc[:, values : 2 * values] + acc[:, 2 * values : 3 * values]
    mean = acc[:, 3 * values : 3 * values + 1] / features
    rstd = 1.0 / jnp.sqrt(square / features - mean * mean + norm_eps)
    velocity = rstd * (hw - mean * consts[0:1, :]) + consts[1:2, :]
    clean = noisy_ref[...].T - sigma_ref[0:1, :] * velocity
    here = h.shape[0] // GRID
    for t in range(here):
        pair = [clean[t * GRID : t * GRID + HALF], clean[t * GRID + HALF : (t + 1) * GRID]]
        rows[step * here + t] = jnp.concatenate(pair, axis=1).astype(bf16)

    @pl.when(step == pl.num_programs(0) - 1)
    def _():
        pl.semaphore_wait(barrier, slabs - 1)
        for d in range(slabs):
            sendbuf[d] = rows[inv_ref[d]]
        copies = []
        for k in range(1, slabs):
            peer = lax.rem(me + k, slabs)
            copy = pltpu.make_async_remote_copy(
                src_ref=sendbuf.at[peer],
                dst_ref=recv.at[me],
                send_sem=send_sem.at[k],
                recv_sem=recv_sem.at[k],
                device_id={"wide": peer},
                device_id_type=MESH,
            )
            copy.start()
            copies.append(copy)
        recv[me] = sendbuf[me]

        def mix(i, carry):
            at = pl.ds(pl.multiple_of(i * 64, 64), 64)
            outer = 0.5 * (g_ref[0, at, :].astype(f32) + g_ref[2, at, :].astype(f32))
            inner = 0.5 * g_ref[1, at, :].astype(f32)
            mixed_ref[0, at, :] = (outer + inner).astype(bf16)
            mixed_ref[1, at, :] = (outer - inner).astype(bf16)
            return carry

        lax.fori_loop(0, g_ref.shape[1] // 64, mix, 0)
        for copy in copies:
            copy.wait_recv()
        for j in range(count):
            ordered[j] = recv[lax.rem(2 * me + slabs - table_ref[j], slabs)]
        edges = []
        for e, (row, peer) in enumerate(((count - 1, lax.rem(me + 1, slabs)), (0, lax.rem(me + slabs - 1, slabs)))):
            copy = pltpu.make_async_remote_copy(
                src_ref=ordered.at[row],
                dst_ref=halo.at[e],
                send_sem=edge_send.at[e],
                recv_sem=edge_recv.at[e],
                device_id={"wide": peer},
                device_id_type=MESH,
            )
            copy.start()
            edges.append(copy)

        lane = lax.broadcasted_iota(jnp.int32, (GRID, 2 * GRID), 1)
        own = lane < GRID
        from_left = (lane // LC) % 2 == 1
        from_upper = (lane // (2 * LC)) % 2 == 1
        zeros = jnp.zeros((8, 2 * GRID), f32)

        def widen(packed, at):
            p = packed.astype(f32)
            swapped = jnp.concatenate([p[:, GRID:], p[:, :GRID]], axis=1)
            twice = jnp.concatenate([jnp.where(own[:HALF], p, swapped), jnp.where(own[:HALF], swapped, p)], axis=0)
            shifted[at, 0:8, :] = zeros
            shifted[at, 8 : 8 + GRID, :] = twice
            shifted[at, 8 + GRID :, :] = zeros
            beside = jnp.where(from_left, shifted[at, 7 : 7 + GRID, :], shifted[at, 9 : 9 + GRID, :])
            wide[at] = jnp.where(own, twice, beside)

        for j in range(count):
            widen(ordered[j], j + 1)
        for copy in edges:
            copy.wait_recv()
        widen(halo[0], 0)
        widen(halo[1], count + 1)
        for i in range(count + 2):
            first = me * count + i - 1 + GRID
            upper = jnp.where(lax.rem(first, GRID) != 0, 1.0, 0.0).astype(f32)
            lower = jnp.where(lax.rem(first + 1, GRID) != 0, 1.0, 0.0).astype(f32)
            above = wide[max(i - 1, 0)] * upper
            below = wide[min(i + 1, count + 1)] * lower
            x_ref[i * GRID : (i + 1) * GRID, 0 : 2 * GRID] = wide[i].astype(bf16)
            x_ref[i * GRID : (i + 1) * GRID, 2 * GRID :] = jnp.where(from_upper, above, below).astype(bf16)
        for copy in copies + edges:
            copy.wait_send()


def relay(hidden, modulation, final_weight, noisy, sigma, inverse, table, g, slabs):
    tokens, features = hidden.shape
    values = final_weight.shape[1]
    count = table.shape[0]
    block = 256
    smem = pl.BlockSpec(memory_space=pltpu.SMEM)
    row = (HALF, 2 * values)
    return pl.pallas_call(
        functools.partial(relay_kernel, slabs, features),
        grid=(tokens // block,),
        in_specs=[
            smem,
            smem,
            pl.BlockSpec((1, values), lambda i: (0, 0)),
            pl.BlockSpec((2, features), lambda i: (0, 0)),
            pl.BlockSpec((values, features), lambda i: (0, 0)),
            pl.BlockSpec((block, features), lambda i: (i, 0)),
            pl.BlockSpec((values, block), lambda i: (0, i)),
            pl.BlockSpec(g.shape, lambda i: (0, 0, 0), pipeline_mode=pl.Buffered(1)),
        ],
        out_specs=[
            pl.BlockSpec(((count + 2) * GRID, 4 * values), lambda i: (0, 0)),
            pl.BlockSpec((2,) + g.shape[1:], lambda i: (0, 0, 0)),
        ],
        out_shape=[
            jax.ShapeDtypeStruct(((count + 2) * GRID, 4 * values), bf16),
            jax.ShapeDtypeStruct((2,) + g.shape[1:], bf16),
        ],
        scratch_shapes=[
            pltpu.VMEM((4 * values, features), bf16),
            pltpu.VMEM((8, values), f32),
            pltpu.VMEM((count,) + row, bf16),
            pltpu.VMEM((slabs,) + row, bf16),
            pltpu.VMEM((slabs,) + row, bf16),
            pltpu.VMEM((count,) + row, bf16),
            pltpu.VMEM((2,) + row, bf16),
            pltpu.VMEM((count + 2, GRID + 16, 2 * values), f32),
            pltpu.VMEM((count + 2, GRID, 2 * values), f32),
            pltpu.SemaphoreType.DMA((slabs,)),
            pltpu.SemaphoreType.DMA((slabs,)),
            pltpu.SemaphoreType.DMA((2,)),
            pltpu.SemaphoreType.DMA((2,)),
        ],
        compiler_params=pltpu.CompilerParams(vmem_limit_bytes=60 << 20, collective_id=0, has_side_effects=True),
        cost_estimate=pl.CostEstimate(flops=2 * tokens * features * 256, bytes_accessed=2 * tokens * features, transcendentals=0),
        name="relay",
    )(inverse, table, jnp.broadcast_to(sigma, (1, values)), modulation, final_weight.T, hidden, noisy.T, g)


def spread_table():
    table = np.zeros((4, 4 * GRID, 9 * LC), np.float32)
    for at in range(4 * GRID):
        lane = at % (2 * GRID)
        a, b, c = (lane // (2 * LC)) % 2, (lane // LC) % 2, lane % LC
        row = a if at < 2 * GRID else (a - 2 if a == 1 else a + 2)
        col = b if lane < GRID else (b - 2 if b == 1 else b + 2)
        for pixel in range(4):
            dr, dc = row - pixel // 2 + 1, col - pixel % 2 + 1
            if 0 <= dr < 3 and 0 <= dc < 3:
                table[pixel, at, (3 * dr + dc) * LC + c] = 1.0
    return table.reshape(-1, 9 * LC)


def decode_kernel(x_ref, spread_ref, win_ref, bin_ref, g_ref, mixed, b1_ref, feat_ref, res_ref, wbig, nat, pad, act, tr_a, tr_b):
    step = pl.program_id(0)
    last = pl.num_programs(0) - 1
    chans = win_ref.shape[1]
    patch = x_ref.shape[1]
    pixel_rows = 2 * CHUNK
    tile = 256

    def setup():
        pad[:, 0:8, :] = jnp.zeros((pixel_rows + 2, 8, chans), f32)
        pad[:, 8 + WPIX :, :] = jnp.zeros((pixel_rows + 2, 8, chans), f32)
        for pixel in range(4):
            part = spread_ref[pixel * patch : (pixel + 1) * patch, :]
            wbig[pixel] = jnp.dot(part, win_ref[...], preferred_element_type=f32).astype(bf16)

    def prepare(tr):
        base = step * CHUNK * GRID
        top = lax.axis_index("wide") * (last * pixel_rows) + step * pixel_rows
        edge = {
            0: jnp.where(lax.rem(top, WPIX) != 0, 1.0, 0.0).astype(f32),
            pixel_rows + 1: jnp.where(lax.rem(top + pixel_rows, WPIX) != 0, 1.0, 0.0).astype(f32),
        }

        def first(start, length, pixel):
            x = x_ref[pl.ds(pl.multiple_of(start, GRID), length), :]
            f = jnp.dot(x, wbig[pixel], preferred_element_type=f32) + bin_ref[...]
            return f.astype(bf16).astype(f32)

        def keep(f, row, b):
            for c in range(chans // 128):
                nat[row, c, pl.ds(b, GRID, stride=2), :] = f[:, c * 128 : (c + 1) * 128]

        def ends(b):
            keep(first(base, GRID, 2 + b), 0, b)
            keep(first(base + (CHUNK + 1) * GRID, GRID, b), pixel_rows + 1, b)

        def middle(pixel):
            f = first(base + GRID, CHUNK * GRID, pixel)
            for t in range(CHUNK):
                keep(f[t * GRID : (t + 1) * GRID], 1 + 2 * t + pixel // 2, pixel % 2)

        def activate(r):
            f = jnp.concatenate([nat[r, c] for c in range(chans // 128)], axis=1)
            if 1 <= r <= pixel_rows:
                feat_ref[r - 1] = f.astype(bf16).T
            half = 0.5 * f
            a = half + half * jnp.tanh(half)
            if r in edge:
                a = a * edge[r]
            pad[r, 8 : 8 + WPIX, :] = a
            act[r, :, chans : 2 * chans] = a.astype(bf16)
            act[r, :, 0:chans] = pad[r, 7 : 7 + WPIX, :].astype(bf16)
            act[r, :, 2 * chans :] = pad[r, 9 : 9 + WPIX, :].astype(bf16)

        def combine(p):
            at = slice(p * WPIX, (p + 1) * WPIX)
            d = [act[2 * p + i] for i in range(4)]
            tr[0, at, :] = d[0] - d[2]
            tr[1, at, :] = d[1] + d[2]
            tr[2, at, :] = d[2] - d[1]
            tr[3, at, :] = d[1] - d[3]

        call = functools.partial
        parts = [call(ends, b) for b in range(2)] + [call(middle, pixel) for pixel in range(4)]
        for r in range(pixel_rows + 2):
            parts.append(call(activate, r))
            if r >= 3 and r % 2 == 1:
                parts.append(call(combine, (r - 3) // 2))
        return parts

    def residual(tr, parts):
        done = 0
        total = 2 * (chans // tile) * (CHUNK * 2)
        slot = 0

        def between():
            nonlocal done, slot
            slot += 1
            while done * total < slot * len(parts) and done < len(parts):
                parts[done]()
                done += 1

        for n in range(chans // tile):
            cols = slice(n * tile, (n + 1) * tile)
            bias = b1_ref[:, cols]
            factors = (g_ref[0, :, cols], mixed[0, :, cols], mixed[1, :, cols], g_ref[2, :, cols])
            m = []
            for k in range(4):
                m.append(jnp.dot(tr[k], factors[k], preferred_element_type=f32))
                between()
                between()
            y0 = m[0] + (m[1] + m[2]) + bias
            y1 = (m[1] - m[2]) - m[3] + bias
            for p in range(CHUNK):
                at = slice(p * WPIX, (p + 1) * WPIX)
                res_ref[2 * p, cols, :] = y0[at].astype(bf16).T
                between()
                res_ref[2 * p + 1, cols, :] = y1[at].astype(bf16).T
                between()

    @pl.when(step == 0)
    def _():
        setup()
        for part in prepare(tr_a):
            part()

    @pl.when((step > 0) & (step < last) & (lax.rem(step, 2) == 1))
    def _():
        residual(tr_a, prepare(tr_b))

    @pl.when((step > 0) & (step < last) & (lax.rem(step, 2) == 0))
    def _():
        residual(tr_b, prepare(tr_a))

    @pl.when((step == last) & (lax.rem(step, 2) == 1))
    def _():
        residual(tr_a, [])

    @pl.when((step == last) & (lax.rem(step, 2) == 0))
    def _():
        residual(tr_b, [])


def decode(x, win, b_in, g, mixed, b1, height):
    chans = win.shape[1]
    rows = 2 * CHUNK
    steps = height // rows
    whole = lambda *shape: pl.BlockSpec(shape, lambda i: (0,) * len(shape), pipeline_mode=pl.Buffered(1))
    shape = jax.ShapeDtypeStruct((height, chans, WPIX), bf16)
    spread = jnp.asarray(spread_table(), bf16)
    return pl.pallas_call(
        decode_kernel,
        grid=(steps + 1,),
        in_specs=[
            whole(*x.shape),
            whole(*spread.shape),
            whole(*win.shape),
            whole(1, chans),
            whole(*g.shape),
            whole(*mixed.shape),
            whole(1, chans),
        ],
        out_specs=[
            pl.BlockSpec((rows, chans, WPIX), lambda i: (jnp.minimum(i, steps - 1), 0, 0)),
            pl.BlockSpec((rows, chans, WPIX), lambda i: (jnp.maximum(i - 1, 0), 0, 0)),
        ],
        out_shape=[shape, shape],
        scratch_shapes=[
            pltpu.VMEM((4, x.shape[1], chans), bf16),
            pltpu.VMEM((rows + 2, chans // 128, WPIX, 128), f32),
            pltpu.VMEM((rows + 2, WPIX + 16, chans), f32),
            pltpu.VMEM((rows + 2, WPIX, 3 * chans), bf16),
            pltpu.VMEM((4, CHUNK * WPIX, 3 * chans), bf16),
            pltpu.VMEM((4, CHUNK * WPIX, 3 * chans), bf16),
        ],
        compiler_params=pltpu.CompilerParams(vmem_limit_bytes=60 << 20),
        cost_estimate=pl.CostEstimate(flops=height * WPIX * 12 * 512 * 512, bytes_accessed=30 << 20, transcendentals=0),
        name="decode",
    )(x, spread, win, b_in[None], g, mixed, b1[None])


def shards(hidden, modulation, final_weight, noisy, step_index, slab_table, conv_in_weight, conv_in_bias, conv1_weight, conv1_bias):
    frac = step_index[0].astype(f32) / STEPS
    sigma = shift_value * frac / (1.0 + (shift_value - 1.0) * frac)
    rows_here = slab_table.shape[0]
    slabs = lax.axis_size("wide")
    slab_ids = jnp.arange(slabs, dtype=jnp.int32)
    local = jnp.arange(rows_here, dtype=jnp.int32)
    inverse = jnp.sum(jnp.where(slab_ids[:, None] == slab_table[None, :], local[None, :], 0), axis=1)
    g = conv1_weight.reshape(3, 3 * conv1_weight.shape[1], conv1_weight.shape[2])
    x, mixed = relay(hidden, modulation, final_weight, noisy, sigma, inverse, slab_table, g, slabs)
    height = 2 * rows_here
    return tuple(decode(x, conv_in_weight, conv_in_bias, g, mixed, conv1_bias, height))


def edge_masks(first_row, count, height):
    global_rows = first_row + jnp.arange(count, dtype=jnp.int32)
    upper = (global_rows % height != 0).astype(f32)
    lower = (global_rows % height != height - 1).astype(f32)
    return (upper, jnp.ones_like(upper), lower)


def split_padded(value, sides, width):
    for axis, dim in sides:
        count, length = (lax.axis_size(axis), value.shape[dim])
        up = [(i, (i + 1) % count) for i in range(count - 1)]
        down = [(j, i) for i, j in up]
        last = lax.slice_in_dim(value, length - width, length, axis=dim)
        first = lax.slice_in_dim(value, 0, width, axis=dim)
        before = lax.ppermute(last, axis, up)
        after = lax.ppermute(first, axis, down)
        value = jnp.concatenate([before, value, after], axis=dim)
    return value


def conv_input_rows(latent, weight, bias, first_row, count, channels):
    width = latent.shape[1] // channels
    planes = latent.reshape(latent.shape[0], width, channels)
    padded = jnp.pad(planes, ((0, 0), (1, 1), (0, 0)))
    masks = edge_masks(first_row, count, width)
    pieces = []
    for row_off in range(3):
        keep = masks[row_off].astype(jnp.bfloat16)[:, None, None]
        for col_off in range(3):
            pieces.append(padded[row_off : row_off + count, col_off : col_off + width, :] * keep)
    patches = jnp.concatenate(pieces, axis=-1)
    return jnp.einsum("rwk,ko->rwo", patches, weight, preferred_element_type=jnp.float32) + bias


def conv_three(total, inputs, weights, first_row, count):
    width = inputs.shape[2]
    padded = jnp.pad(inputs, ((0, 0), (0, 0), (1, 1)))
    masks = edge_masks(first_row, count, width)
    for row_off in range(3):
        keep = masks[row_off][:, None, None]
        for col_off in range(3):
            window = padded[row_off : row_off + count, :, col_off : col_off + width]
            term = jnp.einsum(
                "rkw,ko->row",
                window,
                weights[3 * row_off + col_off],
                preferred_element_type=jnp.float32,
            )
            total = total + keep * term
    return total


def split_shards(
    hidden,
    modulation,
    final_weight,
    noisy,
    step_index,
    slab_table,
    conv_in_weight,
    conv_in_bias,
    conv1_weight,
    conv1_bias,
):
    feats = hidden.astype(jnp.float32)
    weight_f = final_weight.astype(jnp.float32)
    width_all = D
    first_sum, square_sum = lax.psum(
        (jnp.sum(feats, axis=-1), jnp.sum(feats * feats, axis=-1)), "tensor"
    )
    mean = first_sum / width_all
    rstd = 1.0 / jnp.sqrt(square_sum / width_all - mean * mean + norm_eps)
    normed = (feats - mean[:, None]) * rstd[:, None] * (1.0 + modulation[1]) + modulation[0]
    partial_proj = jnp.dot(normed, weight_f, precision=lax.Precision.HIGHEST)
    velocity = lax.psum(partial_proj, "tensor")
    frac = step_index[0].astype(jnp.float32) / STEPS
    sigma = shift_value * frac / (1.0 + (shift_value - 1.0) * frac)
    clean = (noisy - sigma * velocity).astype(jnp.bfloat16)
    rows_here = slab_table.shape[0]
    token_rows = clean.reshape(rows_here, -1)
    slabs = lax.axis_size("wide")
    slab_here = lax.axis_index("wide")
    slab_ids = jnp.arange(slabs, dtype=jnp.int32)
    outgoing = (slab_ids[:, None] == slab_table[None, :]).astype(jnp.bfloat16)
    sendbuf = jnp.dot(outgoing, token_rows, preferred_element_type=jnp.float32).astype(jnp.bfloat16)
    received = lax.all_to_all(sendbuf, "wide", split_axis=0, concat_axis=0, tiled=True)
    source = (2 * slab_here - slab_table) % slabs
    incoming = (source[:, None] == slab_ids[None, :]).astype(jnp.bfloat16)
    slab_rows = jnp.dot(incoming, received, preferred_element_type=jnp.float32).astype(jnp.bfloat16)
    grid_side = GRID
    channels = LC
    pixel_rows = (
        slab_rows.reshape(rows_here, grid_side, 2, 2, channels)
        .transpose(0, 2, 1, 3, 4)
        .reshape(2 * rows_here, 4 * grid_side * channels // 2)
    )
    depth = 2
    latent = split_padded(pixel_rows, (("wide", 0),), depth)
    slab_height = 2 * rows_here
    conv_rows = slab_height + 2 * (depth - 1)
    first_conv = slab_here * slab_height - (depth - 1)
    first = conv_input_rows(latent, conv_in_weight, conv_in_bias, first_conv, conv_rows, channels)
    features = first.astype(jnp.bfloat16).transpose(0, 2, 1)
    activated = jax.nn.silu(features.astype(jnp.float32)).astype(jnp.bfloat16)
    decoder_features = features[depth - 1 : depth - 1 + slab_height]
    local_out = conv_in_weight.shape[1]
    tensor_here = lax.axis_index("tensor")
    pixel_width = activated.shape[2]
    columns = lax.dynamic_slice_in_dim(conv1_weight, tensor_here * local_out, local_out, 2)
    bias_part = lax.dynamic_slice_in_dim(conv1_bias, tensor_here * local_out, local_out, 0)
    first_out = slab_here * slab_height
    gathered = lax.all_gather(activated, "tensor", axis=1, tiled=True)
    start_total = jnp.zeros((slab_height, local_out, pixel_width), jnp.float32)
    summed = conv_three(start_total, gathered, columns, first_out, slab_height)
    residual_branch = (summed + bias_part[None, :, None]).astype(jnp.bfloat16)
    return (decoder_features, residual_branch)


def solution(mesh):
    whole_channels = mesh.shape["tensor"] == 1
    return jax.shard_map(
        shards if whole_channels else split_shards,
        mesh=mesh,
        in_specs=(
            P("wide", "tensor"),
            P(None, "tensor"),
            P("tensor", None),
            P("wide", None),
            P(),
            P("wide"),
            P(None, "tensor"),
            P("tensor"),
            P(),
            P(),
        ),
        out_specs=(P("wide", "tensor", None), P("wide", "tensor", None)),
        check_vma=False,
    )
```
